32 devices in a mesh: groups: 2 (over y), seq: 8 (over z, x), section: 2 (over core).
Axes of the slice: x: 2, y: 2, z: 4, core: 2. Of those that a mesh axis runs over, the one named last changes fastest.
Arguments:
- prompt: bfloat16 [4096, 4096], P(('groups', 'seq'), 'section'), parts along dimension 0, may hold values from -6 to 6
- in_gain: float32 [2, 4096], P(None, 'section'), may hold values from 0.5 to 1.5
- conv_w: bfloat16 [2, 4, 4096], P(None, None, 'section'), may hold values from -3 to 3
- a_log: float32 [2, 64], P(None, 'section'), may hold values from -16 to -2
- out_gain: float32 [2, 4096], P(None, 'section'), may hold values from 0.5 to 1.5
- dt_raw: float32 [2, 4096, 64], P(None, ('groups', 'seq'), 'section'), parts along dimension 1, may hold values from -2.5 to 1.5
- proj: bfloat16 [2, 4096, 2, 256], P(None, ('groups', 'seq'), None, 'section'), parts along dimension 1, may hold values from -6 to 6
Outputs:
- streams: bfloat16 [2, 4096, 4096], P(None, ('groups', 'seq'), 'section'), parts along dimension 1
The draws below stay inside these ranges and needn't reach their ends.
There are 2 independent parts, one for each index of `groups`. The reference program is written for one: setup_inputs(seed, part) draws one part's arguments, and reference() takes and returns one part's arrays. A program takes and returns all parts, laid end to end along the dimension named above; an argument that names none is the same for every part. Nothing has to cross between parts.
All inputs are finite; a program needn't handle non-finite values.
Results may differ from the reference program's by a relative error of at most 0.0064.
Values may be sent and summed in bfloat16 or wider, within the bound.
A program may use at most 256 MiB of HBM per device.

```python
import jax
import jax.numpy as jnp
from jax import lax

D = 4096
HEADS = 64
HEAD_DIM = 64
STATE = 64
GROUPS = 4
CONV = 4
LAYERS = 2
TILE = 256
CHAIN = 2048


def draw_a_log(key, part):
    key = jax.random.fold_in(key, 7)
    pick_key, slow_key, fast_key = jax.random.split(key, 3)
    share = 0.5
    slow = jax.random.uniform(pick_key, (LAYERS, HEADS), jnp.float32) < share
    slow_rate = jax.random.uniform(slow_key, (LAYERS, HEADS), jnp.float32, 0.3, 1.5) / CHAIN
    fast_rate = jax.random.uniform(fast_key, (LAYERS, HEADS), jnp.float32, 0.02, 0.04)
    return jnp.log(jnp.where(slow, slow_rate, fast_rate)).astype(jnp.float32)


def draw_dt_raw(key, part):
    key = jax.random.fold_in(key, 11)
    level_key = jax.random.fold_in(key, 0)
    noise_key = jax.random.fold_in(key, 2)
    blocks = CHAIN // TILE
    level = jax.random.uniform(level_key, (LAYERS, blocks, 1, HEADS), jnp.float32, -1.8, 0.8)
    noise = jax.random.uniform(noise_key, (LAYERS, blocks, TILE, HEADS), jnp.float32, -0.6, 0.6)
    values = jnp.clip(level + noise, -2.5, 1.5)
    return values.reshape(LAYERS, CHAIN, HEADS).astype(jnp.float32)


def steps_of(rng, extent, cuts, smallest, high):
    def one(dim, shards_of):
        steps = jax.random.uniform(jax.random.fold_in(jax.random.fold_in(rng, 6), dim), (shards_of,), jnp.float32, smallest / len(cuts), high / len(cuts))
        return jnp.repeat(jnp.exp(steps), extent[dim] // shards_of).reshape((-1,) + (1,) * (len(extent) - dim - 1))

    gain = one(*cuts[0])
    for cut in cuts[1:]:
        gain = gain * one(*cut)
    return gain


def scatter_about(own_key, extent, deviation, limit, cuts=(), dtype=jnp.bfloat16):
    level = steps_of(own_key, extent, cuts, -0.22, 0.18) if cuts else 1.0
    values = jax.random.normal(own_key, extent, jnp.float32) * deviation * level
    return jnp.minimum(jnp.maximum(values, -limit), limit).astype(dtype)


def setup_inputs(seed: int = 0, part: int = 0) -> dict:
    keys = jax.random.split(jax.random.key(seed), 8)
    part_splits = jax.random.split(jax.random.fold_in(keys[7], part), 8)
    return {
        "prompt": scatter_about(part_splits[0], (CHAIN, D), 1.0, 6.0, ((0, 8), (1, 2))),
        "in_gain": jnp.clip(1.0 + 0.1 * jax.random.normal(keys[1], (LAYERS, D), jnp.float32), 0.5, 1.5),
        "conv_w": scatter_about(keys[2], (LAYERS, CONV, D), CONV ** -0.5, 3.0, ((2, 2),)),
        "a_log": draw_a_log(jax.random.fold_in(keys[7], 71), part),
        "out_gain": jnp.clip(1.0 + 0.1 * jax.random.normal(keys[4], (LAYERS, D), jnp.float32), 0.5, 1.5),
        "dt_raw": draw_dt_raw(jax.random.fold_in(jax.random.fold_in(keys[7], part), 71), part),
        "proj": scatter_about(part_splits[6], (LAYERS, CHAIN, 2, GROUPS * STATE), 1.0, 6.0, ((1, 8), (3, 2))),
    }


EPSILON = 1e-05

def rms_rows(values):
    return values * lax.rsqrt(lax.optimization_barrier(jnp.mean(values * values, axis=-1, keepdims=True)) + EPSILON)

def block_terms(mixed_b, b_groups, c_groups, delta_b, decay_b):
    heads = mixed_b.shape[1]
    per_group = heads // b_groups.shape[1]
    length = mixed_b.shape[0]
    running = jnp.cumsum(decay_b, axis=0)
    scores = jnp.einsum('tgn,sgn->gts', c_groups.astype(jnp.float32), b_groups.astype(jnp.float32))
    scores = jnp.repeat(scores, per_group, axis=0)
    lower = jnp.arange(length)[:, None] >= jnp.arange(length)[None, :]
    gap = running.T[:, :, None] - running.T[:, None, :]
    decay = jnp.where(lower[None], jnp.exp(jnp.where(lower[None], gap, 0.0)), 0.0)
    weights = (decay * delta_b.T[:, None, :] * scores).astype(jnp.bfloat16)
    intra = jnp.einsum('hts,shp->thp', weights.astype(jnp.float32), mixed_b.astype(jnp.float32))
    scaled = (jnp.exp(running[-1][None, :] - running) * delta_b)[:, :, None] * mixed_b.astype(jnp.float32)
    scaled = scaled.astype(jnp.bfloat16)
    b_heads = jnp.repeat(b_groups, per_group, axis=1)
    local_state = jnp.einsum('thp,thn->hpn', scaled.astype(jnp.float32), b_heads.astype(jnp.float32))
    return (running, intra, local_state)

def apply_layer(stream, gain_in, taps, log_rate, gain_out, delta_raw, projected):
    widened = stream.astype(jnp.float32)
    normed = (rms_rows(widened) * gain_in).astype(jnp.bfloat16)
    width = taps.shape[0]
    padded = jnp.concatenate([jnp.zeros((width - 1, D), jnp.bfloat16), normed], axis=0)
    total = jnp.zeros((CHAIN, D), jnp.float32)
    for offset in range(width):
        total = total + taps[offset].astype(jnp.float32) * padded[offset:offset + CHAIN].astype(jnp.float32)
    mixed = jax.nn.silu(total).astype(jnp.bfloat16)
    delta = jax.nn.softplus(delta_raw)
    log_decay = -delta * jnp.exp(log_rate)
    blocks = CHAIN // TILE
    per_group = HEADS // GROUPS
    inputs = (widened.reshape(blocks, TILE, D), mixed.reshape(blocks, TILE, HEADS, HEAD_DIM), projected[:, 0].reshape(blocks, TILE, GROUPS, STATE), projected[:, 1].reshape(blocks, TILE, GROUPS, STATE), delta.reshape(blocks, TILE, HEADS), log_decay.reshape(blocks, TILE, HEADS))

    def advance(entering, pieces):
        rows, mixed_b, b_groups, c_groups, delta_b, decay_b = pieces
        running, intra, local_state = block_terms(mixed_b, b_groups, c_groups, delta_b, decay_b)
        c_heads = jnp.repeat(c_groups, per_group, axis=1).astype(jnp.float32)
        inter = jnp.exp(running)[:, :, None] * jnp.einsum('thn,hpn->thp', c_heads, entering, precision=lax.Precision.HIGHEST)
        combined = intra + inter
        normed_out = rms_rows(combined).reshape(TILE, D)
        result = (rows + normed_out * gain_out).astype(jnp.bfloat16)
        leaving = jnp.exp(running[-1])[:, None, None] * entering + local_state
        return (leaving, result)
    start = jnp.zeros((HEADS, HEAD_DIM, STATE), jnp.float32)
    _, results = lax.scan(advance, start, inputs)
    return results.reshape(CHAIN, D)

def reference(prompt, in_gain, conv_w, a_log, out_gain, dt_raw, proj):
    stream = prompt
    collected = []
    for layer_index in range(LAYERS):
        stream = apply_layer(stream, in_gain[layer_index], conv_w[layer_index], a_log[layer_index], out_gain[layer_index], dt_raw[layer_index], proj[layer_index])
        collected.append(stream)
    return jnp.stack(collected)
```

```python
import functools

import jax
import jax.numpy as jnp
from jax import lax
from jax.experimental import pallas as pl
from jax.experimental.pallas import tpu as pltpu
from jax.sharding import PartitionSpec as P

STATE = 64
WIDE = 256
EPSILON = 1e-05
LOG2E = 1.4426950408889634
MESH = pl.DeviceIdType.MESH
F32 = jnp.float32
BF16 = jnp.bfloat16


def split3(value):
    high = value.astype(BF16)
    rest = value - high.astype(F32)
    middle = rest.astype(BF16)
    low = (rest - middle.astype(F32)).astype(BF16)
    return high, middle, low


def kernel(
    n, sections, prompt, gain_in, conv_w, a_log, gain_out, dt, proj, out,
    r_split, f_split, r_exp, f_exp, q_rows, scores, b_t, c_two,
    pad, mixed, intra, local, squares, scale, scale_halo,
    d_own, d_pair, sum_in, rows_out, rows_in, part_out, part_in,
    z_out, z_in, x_out, x_in,
    d_sem, sum_sem, rows_sem, part_sem, z_send, z_recv, x_send, x_recv,
):
    layers, length, heads = dt.shape
    width = prompt.shape[1]
    head_dim = width // heads
    chunks = width // WIDE
    per_chunk = WIDE // head_dim
    groups = proj.shape[2] // (2 * STATE)
    per_group = chunks // groups
    taps = conv_w.shape[1]

    i = lax.axis_index("seq")
    s = lax.axis_index("section")
    pair = i + 1 - 2 * lax.rem(i, 2)
    first = lax.rem(i, 2) == 0
    has_before = i >= 1
    has_after = i < n - 1
    has_z_in = i >= 2
    has_z_out = i < n - 2

    def cols(c):
        return pl.ds(pl.multiple_of(c * WIDE, WIDE), WIDE)

    barrier = pltpu.get_barrier_semaphore()

    def greet(where):
        pl.semaphore_signal(barrier, inc=1, device_id=where, device_id_type=MESH)

    greet({"section": 1 - s})

    @pl.when(has_before)
    def _():
        greet({"seq": i - 1})
        greet({"seq": i - 1, "section": 1 - s})

    @pl.when(has_after)
    def _():
        greet({"seq": i + 1})
        greet({"seq": i + 1, "section": 1 - s})

    @pl.when(has_z_in)
    def _():
        greet({"seq": i - 2})

    @pl.when(has_z_out)
    def _():
        greet({"seq": i + 2})

    def remote(src, dst, send, recv, where):
        return pltpu.make_async_remote_copy(
            src_ref=src, dst_ref=dst, send_sem=send, recv_sem=recv,
            device_id=where, device_id_type=MESH,
        )

    def decay_copy():
        return remote(d_own, d_pair, d_sem.at[0], d_sem.at[1], {"seq": pair})

    def sum_copy(l):
        return remote(
            squares.at[l], sum_in.at[l], sum_sem.at[l, 0], sum_sem.at[l, 1], {"section": 1 - s}
        )

    def rows_copy(l):
        return remote(
            rows_out.at[l], rows_in.at[l], rows_sem.at[l, 0], rows_sem.at[l, 1], {"seq": i + 1}
        )

    def part_copy(l):
        return remote(
            part_out.at[l], part_in.at[l], part_sem.at[l, 0], part_sem.at[l, 1],
            {"seq": i + 1, "section": 1 - s},
        )

    def z_copy(l, c):
        return remote(
            z_out.at[l, c], z_in.at[l, c], z_send.at[l, c], z_recv.at[l, c], {"seq": i + 2}
        )

    def x_copy(l, c):
        return remote(
            x_out.at[l, c], x_in.at[l, c], x_send.at[l, c], x_recv.at[l, c], {"seq": pair}
        )

    def send_sums(l):
        part_out[l] = squares[l, length - 8 :, :]
        sum_copy(l).start()

        @pl.when(has_after)
        def _():
            rows_copy(l).start()
            part_copy(l).start()

    def fold(value):
        total = value[:, :128]
        for k in range(1, value.shape[1] // 128):
            total = total + value[:, k * 128 : (k + 1) * 128]
        return total

    squares[0] = jnp.zeros(squares.shape[1:], F32)

    @pl.loop(0, chunks)
    def _(c):
        h = prompt[:, cols(c)].astype(F32)
        squares[0] += fold(h * h)
        rows_out[0, :, cols(c)] = prompt[length - 16 :, cols(c)]

    @pl.when(i == 0)
    def _():
        rows_in[...] = jnp.zeros(rows_in.shape, BF16)
        part_in[...] = jnp.zeros(part_in.shape, F32)

    @pl.when(i < 2)
    def _():
        z_in[...] = jnp.zeros(z_in.shape, BF16)

    one = jnp.int32(1)
    zero = jnp.int32(0)
    expected = (
        1
        + 2 * jnp.where(has_before, one, zero)
        + 2 * jnp.where(has_after, one, zero)
        + jnp.where(has_z_in, one, zero)
        + jnp.where(has_z_out, one, zero)
    )
    pl.semaphore_wait(barrier, expected)
    send_sums(0)

    def wide(pieces):
        lanes = sum(p.shape[1] for p in pieces)
        rest = jnp.zeros((pieces[0].shape[0], 128 - lanes), pieces[0].dtype)
        return jnp.concatenate(pieces + [rest], axis=1)

    raw = wide([dt[l] for l in range(layers)])
    rate = jnp.exp(wide([a_log[l : l + 1, :] for l in range(layers)])) * LOG2E
    delta = jnp.maximum(raw, 0.0) + jnp.log(1.0 + jnp.exp(-jnp.abs(raw)))
    step = -delta * rate
    t_of = lax.broadcasted_iota(jnp.int32, (length, length), 0)
    s_of = lax.broadcasted_iota(jnp.int32, (length, length), 1)
    lower = t_of >= s_of
    running = jnp.dot(
        lower.astype(F32), step, preferred_element_type=F32, precision=lax.Precision.HIGHEST
    )
    behind = running - jnp.log(delta) * LOG2E
    ahead = running[length - 1 :, :] - behind
    turned = behind.T
    for lc in range(layers * chunks):
        q_rows[lc, :per_chunk, :] = turned[lc * per_chunk : (lc + 1) * per_chunk, :]
    for l in range(layers):
        mine = slice(l * heads, (l + 1) * heads)
        r_split[l] = wide([p.astype(F32) for p in split3(running[:, mine])]).astype(BF16)
        f_split[l] = wide([p.astype(F32) for p in split3(ahead[:, mine])]).astype(BF16)

    @pl.loop(0, layers * chunks)
    def _(lc):
        l = lc // chunks
        c = lax.rem(lc, chunks)
        row = lax.broadcasted_iota(jnp.int32, (128, WIDE), 0)
        lane = lax.broadcasted_iota(jnp.int32, (128, WIDE), 1)
        hit = (lax.rem(row, heads) == c * per_chunk + lane // head_dim) & (row < 3 * heads)
        pick = hit.astype(F32).astype(BF16)
        spread = jnp.dot(r_split[l], pick, preferred_element_type=F32)
        r_exp[lc] = spread
        d_own[pl.ds(lc, 1), :] = jnp.exp2(spread[length - 1 :, :])
        f_exp[lc] = jnp.exp2(jnp.dot(f_split[l], pick, preferred_element_type=F32))

    decay_copy().start()

    for l in range(layers):
        half = groups * STATE
        b_all = proj[l, :, :half].astype(F32)
        c_all = proj[l, :, half:].astype(F32)
        turned_b = b_all.T.astype(BF16)
        b_t[l] = turned_b
        for g in range(groups):
            c_g = c_all[:, g * STATE : (g + 1) * STATE]
            c_two[l * groups + g] = jnp.concatenate([c_g, c_g], axis=1).astype(BF16)
            both = jnp.dot(
                c_g.astype(BF16), turned_b[g * STATE : (g + 1) * STATE], preferred_element_type=F32
            )
            scores[l * groups + g] = jnp.where(lower, both, 0.0)

    head_of = lax.broadcasted_iota(jnp.int32, (length, WIDE), 1) // head_dim

    for l in range(layers):
        sum_copy(l).wait_recv()
        total = jnp.sum(squares[l] + sum_in[l], axis=1, keepdims=True)
        scale[...] = jnp.broadcast_to(
            lax.rsqrt(total / (width * sections) + EPSILON), scale.shape
        )

        @pl.when(has_before)
        def _():
            rows_copy(l).wait_recv()
            part_copy(l).wait_recv()

        halo_sum = part_in[l]
        for c in range(chunks):
            h = rows_in[l, :, c * WIDE : (c + 1) * WIDE].astype(F32)[8:]
            halo_sum = halo_sum + fold(h * h)
        halo_total = jnp.sum(halo_sum, axis=1, keepdims=True)
        scale_halo[...] = jnp.broadcast_to(
            lax.rsqrt(halo_total / (width * sections) + EPSILON), scale_halo.shape
        )
        if l == 0:
            decay_copy().wait_recv()

        def source(c):
            return prompt[:, cols(c)] if l == 0 else out[l - 1, :, cols(c)]

        def double(value):
            return jnp.concatenate([value] * (WIDE // 128), axis=1)

        def coefficients(c):
            own = d_own[pl.ds(l * chunks + c, 1), :]
            other = d_pair[pl.ds(l * chunks + c, 1), :]
            return own, other

        @pl.loop(0, chunks)
        def _(c):
            gain = gain_in[l : l + 1, cols(c)]
            h = source(c).astype(F32)
            normed = (h * double(scale[...]) * gain).astype(BF16).astype(F32)
            before = rows_in[l, :, cols(c)].astype(F32)[8:]
            pad[:8, :] = (before * double(scale_halo[...]) * gain).astype(BF16).astype(F32)
            pad[8:, :] = normed
            weight = conv_w[l, :, cols(c)].astype(F32)
            total = weight[taps - 1 : taps, :] * normed
            for k in range(taps - 1):
                start = 8 - (taps - 1) + k
                total = total + weight[k : k + 1, :] * pad[start : start + length, :]
            half = 0.5 * total
            here = (half + half * jnp.tanh(half)).astype(BF16)
            mixed[c] = here
            scaled = (f_exp[l * chunks + c] * here.astype(F32)).astype(BF16)
            g = c // per_group
            rows = pl.ds(pl.multiple_of(g * STATE, STATE), STATE)
            state = jnp.dot(b_t[l, rows, :], scaled, preferred_element_type=F32)
            local[c] = state
            own, other = coefficients(c)

            @pl.when(i < 2)
            def _():
                z_out[l, c] = (jnp.where(first, other, 1.0) * state).astype(BF16)

                @pl.when(has_z_out)
                def _():
                    z_copy(l, c).start()

        if l + 1 < layers:
            squares[l + 1] = jnp.zeros(squares.shape[1:], F32)

        def finish(c):
            x_copy(l, c).wait_recv()
            own, other = coefficients(c)
            g = l * groups + c // per_group
            entering = jnp.where(first, 1.0, other) * z_in[l, c].astype(F32) + x_in[l, c].astype(F32)
            high = entering.astype(BF16)
            low = (entering - high.astype(F32)).astype(BF16)
            inter = jnp.dot(
                c_two[g], jnp.concatenate([high, low], axis=0), preferred_element_type=F32
            )
            y = intra[c] + jnp.exp2(r_exp[l * chunks + c]) * inter
            row = lax.broadcasted_iota(jnp.int32, (WIDE, WIDE), 0) // head_dim
            same = (row == lax.broadcasted_iota(jnp.int32, (WIDE, WIDE), 1) // head_dim)
            power = jnp.dot(
                (y * y).astype(BF16), same.astype(F32).astype(BF16), preferred_element_type=F32
            )
            scaled = y * lax.rsqrt(power * (1.0 / head_dim) + EPSILON)
            after = (source(c).astype(F32) + scaled * gain_out[l : l + 1, cols(c)]).astype(BF16)
            out[l, :, cols(c)] = after
            if l + 1 < layers:
                rows_out[l + 1, :, cols(c)] = after[length - 16 :, :]
                wide_after = after.astype(F32)
                squares[l + 1] += fold(wide_after * wide_after)

        @pl.loop(0, chunks)
        def _(c):
            lc = l * chunks + c
            g = l * groups + c // per_group
            here = mixed[c]
            left, right = [], []
            for h in range(per_chunk):
                column = r_exp[lc, :, h * head_dim : h * head_dim + 1]
                decay = jnp.exp2(column - q_rows[lc, h : h + 1, :])
                left.append((decay * scores[g]).astype(BF16))
                right.append(jnp.where(head_of == h, here, jnp.zeros_like(here)))
            intra[c] = jnp.dot(
                jnp.concatenate(left, axis=1),
                jnp.concatenate(right, axis=0),
                preferred_element_type=F32,
            )
            own, other = coefficients(c)
            state = local[c]

            @pl.when(has_z_in)
            def _():
                z_copy(l, c).wait_recv()

                @pl.when(has_z_out)
                def _():
                    z_out[l, c] = (
                        own * other * z_in[l, c].astype(F32) + jnp.where(first, other, 1.0) * state
                    ).astype(BF16)
                    z_copy(l, c).start()

            arrived = z_in[l, c].astype(F32)
            x_out[l, c] = jnp.where(first, own * arrived + state, arrived).astype(BF16)
            x_copy(l, c).start()

            @pl.when(c >= 1)
            def _():
                finish(c - 1)

        finish(jnp.int32(chunks - 1))
        if l + 1 < layers:
            send_sums(l + 1)

    decay_copy().wait_send()
    for l in range(layers):
        sum_copy(l).wait_send()

        @pl.when(has_after)
        def _():
            rows_copy(l).wait_send()
            part_copy(l).wait_send()

        @pl.loop(0, chunks)
        def _(c):
            x_copy(l, c).wait_send()

            @pl.when(has_z_out)
            def _():
                z_copy(l, c).wait_send()


def local_part(n, sections, prompt, in_gain, conv_w, a_log, out_gain, dt_raw, proj):
    length, width = prompt.shape
    layers, _, heads = dt_raw.shape
    lanes = proj.shape[2] * proj.shape[3]
    chunks = width // WIDE
    groups = proj.shape[3] // STATE
    vmem = pltpu.VMEM
    dma = pltpu.SemaphoreType.DMA
    lc = layers * chunks
    scratch = [
        vmem((layers, length, 128), BF16),
        vmem((layers, length, 128), BF16),
        vmem((lc, length, WIDE), F32),
        vmem((lc, length, WIDE), F32),
        vmem((lc, 8, length), F32),
        vmem((layers * groups, length, length), F32),
        vmem((layers, groups * STATE, length), BF16),
        vmem((layers * groups, length, 2 * STATE), BF16),
        vmem((length + 8, WIDE), F32),
        vmem((chunks, length, WIDE), BF16),
        vmem((chunks, length, WIDE), F32),
        vmem((chunks, STATE, WIDE), F32),
        vmem((layers, length, 128), F32),
        vmem((length, 128), F32),
        vmem((8, 128), F32),
        vmem((lc, WIDE), F32),
        vmem((lc, WIDE), F32),
        vmem((layers, length, 128), F32),
        vmem((layers, 16, width), BF16),
        vmem((layers, 16, width), BF16),
        vmem((layers, 8, 128), F32),
        vmem((layers, 8, 128), F32),
        vmem((layers, chunks, STATE, WIDE), BF16),
        vmem((layers, chunks, STATE, WIDE), BF16),
        vmem((layers, chunks, STATE, WIDE), BF16),
        vmem((layers, chunks, STATE, WIDE), BF16),
        dma((2,)),
        dma((layers, 2)),
        dma((layers, 2)),
        dma((layers, 2)),
        dma((layers, chunks)),
        dma((layers, chunks)),
        dma((layers, chunks)),
        dma((layers, chunks)),
    ]
    return pl.pallas_call(
        functools.partial(kernel, n, sections),
        out_shape=jax.ShapeDtypeStruct((layers, length, width), BF16),
        in_specs=[pl.BlockSpec(memory_space=pltpu.VMEM)] * 7,
        out_specs=pl.BlockSpec(memory_space=pltpu.VMEM),
        scratch_shapes=scratch,
        compiler_params=pltpu.CompilerParams(
            collective_id=0, has_side_effects=True, vmem_limit_bytes=48 * 1024 * 1024
        ),
    )(prompt, in_gain, conv_w, a_log, out_gain, dt_raw, proj.reshape(layers, length, lanes))


def solution(mesh):
    in_specs = (
        P(("groups", "seq"), "section"),
        P(None, "section"),
        P(None, None, "section"),
        P(None, "section"),
        P(None, "section"),
        P(None, ("groups", "seq"), "section"),
        P(None, ("groups", "seq"), None, "section"),
    )
    out_specs = P(None, ("groups", "seq"), "section")
    part = functools.partial(local_part, mesh.shape["seq"], mesh.shape["section"])
    return jax.shard_map(part, mesh=mesh, in_specs=in_specs, out_specs=out_specs, check_vma=False)
```

```python
import functools

import jax
import jax.numpy as jnp
from jax import lax
from jax.experimental import pallas as pl
from jax.experimental.pallas import tpu as pltpu
from jax.sharding import PartitionSpec as P

STATE = 64
WIDE = 256
EPSILON = 1e-05
LOG2E = 1.4426950408889634
MESH = pl.DeviceIdType.MESH
F32 = jnp.float32
BF16 = jnp.bfloat16


def split3(value):
    high = value.astype(BF16)
    rest = value - high.astype(F32)
    middle = rest.astype(BF16)
    low = (rest - middle.astype(F32)).astype(BF16)
    return high, middle, low


def kernel(
    n, sections, prompt_h, gain_in_h, conv_w_h, a_log_h, gain_out_h, dt_h, proj_h, out,
    prompt, gain_in, conv_w, a_log, gain_out, dt, proj, proj_wide, in_sem,
    r_split, f_split, r_exp, f_exp, q_rows, scores, b_t, c_two,
    pad, mixed, intra, local, squares, scale, scale_halo,
    d_own, d_pair, sum_in, rows_out, rows_in, part_out, part_in,
    z_out, z_in, x_out, x_in,
    d_sem, sum_sem, rows_sem, part_sem, z_send, z_recv, x_send, x_recv,
):
    layers, heads, length = dt.shape
    width = prompt.shape[1]
    head_dim = width // heads
    chunks = width // WIDE
    per_chunk = WIDE // head_dim
    groups = proj.shape[2] // STATE
    per_group = chunks // groups
    taps = conv_w.shape[1]

    i = lax.axis_index("seq")
    s = lax.axis_index("section")
    pair = i + 1 - 2 * lax.rem(i, 2)
    first = lax.rem(i, 2) == 0
    has_before = i >= 1
    has_after = i < n - 1
    has_z_in = i >= 2
    has_z_out = i < n - 2

    def cols(c):
        return pl.ds(pl.multiple_of(c * WIDE, WIDE), WIDE)

    arrivals = {}
    for k, (there, here) in enumerate(
        (
            (prompt_h, prompt), (dt_h, dt), (a_log_h, a_log), (proj_h, proj),
            (gain_in_h, gain_in), (conv_w_h, conv_w), (gain_out_h, gain_out),
        )
    ):
        arrivals[k] = pltpu.make_async_copy(there, here, in_sem.at[k])
        arrivals[k].start()

    barrier = pltpu.get_barrier_semaphore()

    def greet(where):
        pl.semaphore_signal(barrier, inc=1, device_id=where, device_id_type=MESH)

    greet({"section": 1 - s})

    @pl.when(has_before)
    def _():
        greet({"seq": i - 1})
        greet({"seq": i - 1, "section": 1 - s})

    @pl.when(has_after)
    def _():
        greet({"seq": i + 1})
        greet({"seq": i + 1, "section": 1 - s})

    @pl.when(has_z_in)
    def _():
        greet({"seq": i - 2})

    @pl.when(has_z_out)
    def _():
        greet({"seq": i + 2})

    def remote(src, dst, send, recv, where):
        return pltpu.make_async_remote_copy(
            src_ref=src, dst_ref=dst, send_sem=send, recv_sem=recv,
            device_id=where, device_id_type=MESH,
        )

    def decay_copy(l):
        return remote(d_own.at[l], d_pair.at[l], d_sem.at[l, 0], d_sem.at[l, 1], {"seq": pair})

    def sum_copy(l):
        return remote(
            squares.at[l], sum_in.at[l], sum_sem.at[l, 0], sum_sem.at[l, 1], {"section": 1 - s}
        )

    def rows_copy(l):
        return remote(
            rows_out.at[l], rows_in.at[l], rows_sem.at[l, 0], rows_sem.at[l, 1], {"seq": i + 1}
        )

    def part_copy(l):
        return remote(
            part_out.at[l], part_in.at[l], part_sem.at[l, 0], part_sem.at[l, 1],
            {"seq": i + 1, "section": 1 - s},
        )

    def z_copy(l, c):
        return remote(
            z_out.at[l, c], z_in.at[l, c], z_send.at[l, c], z_recv.at[l, c], {"seq": i + 2}
        )

    def x_copy(l, c):
        return remote(
            x_out.at[l, c], x_in.at[l, c], x_send.at[l, c], x_recv.at[l, c], {"seq": pair}
        )

    def send_sums(l):
        part_out[l] = squares[l, length - 8 :, :]
        sum_copy(l).start()

        @pl.when(has_after)
        def _():
            rows_copy(l).start()
            part_copy(l).start()

    def fold(value):
        total = value[:, :128]
        for k in range(1, value.shape[1] // 128):
            total = total + value[:, k * 128 : (k + 1) * 128]
        return total

    squares[0] = jnp.zeros(squares.shape[1:], F32)
    arrivals[0].wait()

    @pl.loop(0, chunks)
    def _(c):
        h = prompt[:, cols(c)].astype(F32)
        squares[0] += fold(h * h)
        rows_out[0, :, cols(c)] = prompt[length - 16 :, cols(c)]

    @pl.when(i == 0)
    def _():
        rows_in[...] = jnp.zeros(rows_in.shape, BF16)
        part_in[...] = jnp.zeros(part_in.shape, F32)

    @pl.when(i < 2)
    def _():
        z_in[...] = jnp.zeros(z_in.shape, BF16)

    one = jnp.int32(1)
    zero = jnp.int32(0)
    expected = (
        1
        + 2 * jnp.where(has_before, one, zero)
        + 2 * jnp.where(has_after, one, zero)
        + jnp.where(has_z_in, one, zero)
        + jnp.where(has_z_out, one, zero)
    )
    pl.semaphore_wait(barrier, expected)
    send_sums(0)

    for k in range(1, len(arrivals)):
        arrivals[k].wait()

    def wide(pieces):
        lanes = sum(p.shape[1] for p in pieces)
        rest = jnp.zeros((pieces[0].shape[0], 128 - lanes), pieces[0].dtype)
        return jnp.concatenate(pieces + [rest], axis=1)

    idle = jnp.zeros((128 - layers * heads, length), F32)
    raw = jnp.concatenate([dt[l] for l in range(layers)] + [idle], axis=0).T
    rate = jnp.exp(wide([a_log[l : l + 1, :] for l in range(layers)])) * LOG2E
    delta = jnp.maximum(raw, 0.0) + jnp.log(1.0 + jnp.exp(-jnp.abs(raw)))
    step = -delta * rate
    t_of = lax.broadcasted_iota(jnp.int32, (length, length), 0)
    s_of = lax.broadcasted_iota(jnp.int32, (length, length), 1)
    lower = t_of >= s_of
    running = jnp.dot(
        lower.astype(F32), step, preferred_element_type=F32, precision=lax.Precision.HIGHEST
    )
    behind = running - jnp.log(delta) * LOG2E
    ahead = running[length - 1 :, :] - behind
    turned = behind.T
    for lc in range(layers * chunks):
        q_rows[lc, :per_chunk, :] = turned[lc * per_chunk : (lc + 1) * per_chunk, :]
    for l in range(layers):
        mine = slice(l * heads, (l + 1) * heads)
        r_split[l] = wide([p.astype(F32) for p in split3(running[:, mine])]).astype(BF16)
        f_split[l] = wide([p.astype(F32) for p in split3(ahead[:, mine])]).astype(BF16)

    def spread_steps(l, c):
        lc = l * chunks + c
        row = lax.broadcasted_iota(jnp.int32, (128, WIDE), 0)
        lane = lax.broadcasted_iota(jnp.int32, (128, WIDE), 1)
        hit = (lax.rem(row, heads) == c * per_chunk + lane // head_dim) & (row < 3 * heads)
        pick = hit.astype(F32).astype(BF16)
        spread = jnp.dot(r_split[l], pick, preferred_element_type=F32)
        r_exp[lc] = spread
        d_own[l, pl.ds(c, 1), :] = jnp.exp2(spread[length - 1 :, :])
        f_exp[lc] = jnp.exp2(jnp.dot(f_split[l], pick, preferred_element_type=F32))

    @pl.loop(0, chunks)
    def _(c):
        spread_steps(0, c)

    decay_copy(0).start()

    for l in range(layers):
        proj_wide[...] = proj[l].astype(F32)
        b_all = proj_wide[pl.ds(0, length, stride=2), :]
        c_all = proj_wide[pl.ds(1, length, stride=2), :]
        turned_b = b_all.T.astype(BF16)
        b_t[l] = turned_b
        for g in range(groups):
            c_g = c_all[:, g * STATE : (g + 1) * STATE]
            c_two[l * groups + g] = jnp.concatenate([c_g, c_g], axis=1).astype(BF16)
            both = jnp.dot(
                c_g.astype(BF16), turned_b[g * STATE : (g + 1) * STATE], preferred_element_type=F32
            )
            scores[l * groups + g] = jnp.where(lower, both, 0.0)

    head_of = lax.broadcasted_iota(jnp.int32, (length, WIDE), 1) // head_dim

    for l in range(layers):
        sum_copy(l).wait_recv()
        total = jnp.sum(squares[l] + sum_in[l], axis=1, keepdims=True)
        scale[...] = jnp.broadcast_to(
            lax.rsqrt(total / (width * sections) + EPSILON), scale.shape
        )

        @pl.when(has_before)
        def _():
            rows_copy(l).wait_recv()
            part_copy(l).wait_recv()

        halo_sum = part_in[l]
        for c in range(chunks):
            h = rows_in[l, :, c * WIDE : (c + 1) * WIDE].astype(F32)[8:]
            halo_sum = halo_sum + fold(h * h)
        halo_total = jnp.sum(halo_sum, axis=1, keepdims=True)
        scale_halo[...] = jnp.broadcast_to(
            lax.rsqrt(halo_total / (width * sections) + EPSILON), scale_halo.shape
        )
        decay_copy(l).wait_recv()

        def source(c):
            return prompt[:, cols(c)] if l == 0 else out[l - 1, :, cols(c)]

        def double(value):
            return jnp.concatenate([value] * (WIDE // 128), axis=1)

        def coefficients(c):
            own = d_own[l, pl.ds(c, 1), :]
            other = d_pair[l, pl.ds(c, 1), :]
            return own, other

        @pl.loop(0, chunks)
        def _(c):
            gain = gain_in[l : l + 1, cols(c)]
            h = source(c).astype(F32)
            normed = (h * double(scale[...]) * gain).astype(BF16).astype(F32)
            before = rows_in[l, :, cols(c)].astype(F32)[8:]
            pad[:8, :] = (before * double(scale_halo[...]) * gain).astype(BF16).astype(F32)
            pad[8:, :] = normed
            weight = conv_w[l, :, cols(c)].astype(F32)
            total = weight[taps - 1 : taps, :] * normed
            for k in range(taps - 1):
                start = 8 - (taps - 1) + k
                total = total + weight[k : k + 1, :] * pad[start : start + length, :]
            half = 0.5 * total
            here = (half + half * jnp.tanh(half)).astype(BF16)
            mixed[c] = here
            scaled = (f_exp[l * chunks + c] * here.astype(F32)).astype(BF16)
            g = c // per_group
            rows = pl.ds(pl.multiple_of(g * STATE, STATE), STATE)
            state = jnp.dot(b_t[l, rows, :], scaled, preferred_element_type=F32)
            local[c] = state
            own, other = coefficients(c)

            @pl.when(i < 2)
            def _():
                z_out[l, c] = (jnp.where(first, other, 1.0) * state).astype(BF16)

                @pl.when(has_z_out)
                def _():
                    z_copy(l, c).start()

        if l + 1 < layers:
            squares[l + 1] = jnp.zeros(squares.shape[1:], F32)

        def finish(c):
            x_copy(l, c).wait_recv()
            own, other = coefficients(c)
            g = l * groups + c // per_group
            entering = jnp.where(first, 1.0, other) * z_in[l, c].astype(F32) + x_in[l, c].astype(F32)
            high = entering.astype(BF16)
            low = (entering - high.astype(F32)).astype(BF16)
            inter = jnp.dot(
                c_two[g], jnp.concatenate([high, low], axis=0), preferred_element_type=F32
            )
            y = intra[c] + jnp.exp2(r_exp[l * chunks + c]) * inter
            row = lax.broadcasted_iota(jnp.int32, (WIDE, WIDE), 0) // head_dim
            same = (row == lax.broadcasted_iota(jnp.int32, (WIDE, WIDE), 1) // head_dim)
            power = jnp.dot(
                (y * y).astype(BF16), same.astype(F32).astype(BF16), preferred_element_type=F32
            )
            scaled = y * lax.rsqrt(power * (1.0 / head_dim) + EPSILON)
            after = (source(c).astype(F32) + scaled * gain_out[l : l + 1, cols(c)]).astype(BF16)
            out[l, :, cols(c)] = after
            if l + 1 < layers:
                rows_out[l + 1, :, cols(c)] = after[length - 16 :, :]
                wide_after = after.astype(F32)
                squares[l + 1] += fold(wide_after * wide_after)

        @pl.loop(0, chunks)
        def _(c):
            lc = l * chunks + c
            g = l * groups + c // per_group
            here = mixed[c]
            left, right = [], []
            for h in range(per_chunk):
                column = r_exp[lc, :, h * head_dim : h * head_dim + 1]
                decay = jnp.exp2(column - q_rows[lc, h : h + 1, :])
                left.append((decay * scores[g]).astype(BF16))
                right.append(jnp.where(head_of == h, here, jnp.zeros_like(here)))
            intra[c] = jnp.dot(
                jnp.concatenate(left, axis=1),
                jnp.concatenate(right, axis=0),
                preferred_element_type=F32,
            )
            own, other = coefficients(c)
            state = local[c]

            @pl.when(has_z_in)
            def _():
                z_copy(l, c).wait_recv()

                @pl.when(has_z_out)
                def _():
                    z_out[l, c] = (
                        own * other * z_in[l, c].astype(F32) + jnp.where(first, other, 1.0) * state
                    ).astype(BF16)
                    z_copy(l, c).start()

            arrived = z_in[l, c].astype(F32)
            x_out[l, c] = jnp.where(first, own * arrived + state, arrived).astype(BF16)
            x_copy(l, c).start()

            if l + 1 < layers:
                spread_steps(l + 1, c)

        if l + 1 < layers:
            decay_copy(l + 1).start()

        @pl.loop(0, chunks)
        def _(c):
            finish(c)

        if l + 1 < layers:
            send_sums(l + 1)

    for l in range(layers):
        decay_copy(l).wait_send()
        sum_copy(l).wait_send()

        @pl.when(has_after)
        def _():
            rows_copy(l).wait_send()
            part_copy(l).wait_send()

        @pl.loop(0, chunks)
        def _(c):
            x_copy(l, c).wait_send()

            @pl.when(has_z_out)
            def _():
                z_copy(l, c).wait_send()


def local_part(n, sections, prompt, in_gain, conv_w, a_log, out_gain, dt_raw, proj):
    length, width = prompt.shape
    layers, _, heads = dt_raw.shape
    operands = (
        prompt, in_gain, conv_w, a_log, out_gain,
        dt_raw.transpose(0, 2, 1), proj.reshape(layers, 2 * length, proj.shape[3]),
    )
    chunks = width // WIDE
    groups = proj.shape[3] // STATE
    vmem = pltpu.VMEM
    dma = pltpu.SemaphoreType.DMA
    lc = layers * chunks
    scratch = [vmem(value.shape, value.dtype) for value in operands] + [
        vmem((2 * length, proj.shape[3]), F32),
        dma((len(operands),)),
        vmem((layers, length, 128), BF16),
        vmem((layers, length, 128), BF16),
        vmem((lc, length, WIDE), F32),
        vmem((lc, length, WIDE), F32),
        vmem((lc, 8, length), F32),
        vmem((layers * groups, length, length), F32),
        vmem((layers, groups * STATE, length), BF16),
        vmem((layers * groups, length, 2 * STATE), BF16),
        vmem((length + 8, WIDE), F32),
        vmem((chunks, length, WIDE), BF16),
        vmem((chunks, length, WIDE), F32),
        vmem((chunks, STATE, WIDE), F32),
        vmem((layers, length, 128), F32),
        vmem((length, 128), F32),
        vmem((8, 128), F32),
        vmem((layers, chunks, WIDE), F32),
        vmem((layers, chunks, WIDE), F32),
        vmem((layers, length, 128), F32),
        vmem((layers, 16, width), BF16),
        vmem((layers, 16, width), BF16),
        vmem((layers, 8, 128), F32),
        vmem((layers, 8, 128), F32),
        vmem((layers, chunks, STATE, WIDE), BF16),
        vmem((layers, chunks, STATE, WIDE), BF16),
        vmem((layers, chunks, STATE, WIDE), BF16),
        vmem((layers, chunks, STATE, WIDE), BF16),
        dma((layers, 2)),
        dma((layers, 2)),
        dma((layers, 2)),
        dma((layers, 2)),
        dma((layers, chunks)),
        dma((layers, chunks)),
        dma((layers, chunks)),
        dma((layers, chunks)),
    ]
    return pl.pallas_call(
        functools.partial(kernel, n, sections),
        out_shape=jax.ShapeDtypeStruct((layers, length, width), BF16),
        in_specs=[pl.BlockSpec(memory_space=pltpu.HBM)] * len(operands),
        out_specs=pl.BlockSpec(memory_space=pltpu.VMEM),
        scratch_shapes=scratch,
        compiler_params=pltpu.CompilerParams(
            collective_id=0, has_side_effects=True, vmem_limit_bytes=60 * 1024 * 1024
        ),
    )(*operands)


def solution(mesh):
    in_specs = (
        P(("groups", "seq"), "section"),
        P(None, "section"),
        P(None, None, "section"),
        P(None, "section"),
        P(None, "section"),
        P(None, ("groups", "seq"), "section"),
        P(None, ("groups", "seq"), None, "section"),
    )
    out_specs = P(None, ("groups", "seq"), "section")
    part = functools.partial(local_part, mesh.shape["seq"], mesh.shape["section"])
    return jax.shard_map(part, mesh=mesh, in_specs=in_specs, out_specs=out_specs, check_vma=False)
```

```python
import functools

import jax
import jax.numpy as jnp
from jax import lax
from jax.experimental import pallas as pl
from jax.experimental.pallas import tpu as pltpu
from jax.sharding import PartitionSpec as P

STATE = 64
WIDE = 256
EPSILON = 1e-05
LOG2E = 1.4426950408889634
MESH = pl.DeviceIdType.MESH
F32 = jnp.float32
BF16 = jnp.bfloat16


def split3(value):
    high = value.astype(BF16)
    rest = value - high.astype(F32)
    middle = rest.astype(BF16)
    low = (rest - middle.astype(F32)).astype(BF16)
    return high, middle, low


def kernel(
    n, sections, prompt_h, gain_in_h, conv_w_h, a_log_h, gain_out_h, dt_h, proj_h, out,
    prompt, gain_in, conv_w, a_log, gain_out, dt, proj, proj_wide, in_sem,
    r_split, f_split, r_exp, f_exp, q_rows, scores, b_t, c_two,
    pad, mixed, intra, local, squares, scale, scale_halo,
    d_own, d_pair, sum_in, rows_out, rows_in, part_out, part_in,
    z_out, z_in, x_out, x_in,
    d_sem, sum_sem, rows_sem, part_sem, z_send, z_recv, x_send, x_recv,
):
    layers, heads, length = dt.shape
    width = prompt.shape[1]
    head_dim = width // heads
    chunks = width // WIDE
    per_chunk = WIDE // head_dim
    groups = proj.shape[2] // STATE
    per_group = chunks // groups
    taps = conv_w.shape[1]

    i = lax.axis_index("seq")
    s = lax.axis_index("section")
    pair = i + 1 - 2 * lax.rem(i, 2)
    first = lax.rem(i, 2) == 0
    has_before = i >= 1
    has_after = i < n - 1
    has_z_in = i >= 2
    has_z_out = i < n - 2

    def cols(c):
        return pl.ds(pl.multiple_of(c * WIDE, WIDE), WIDE)

    arrivals = {}
    for k, (there, here) in enumerate(
        (
            (prompt_h, prompt), (dt_h, dt), (a_log_h, a_log), (proj_h, proj),
            (gain_in_h, gain_in), (conv_w_h, conv_w), (gain_out_h, gain_out),
        )
    ):
        arrivals[k] = pltpu.make_async_copy(there, here, in_sem.at[k])
        arrivals[k].start()

    barrier = pltpu.get_barrier_semaphore()

    def greet(where):
        pl.semaphore_signal(barrier, inc=1, device_id=where, device_id_type=MESH)

    greet({"section": 1 - s})

    @pl.when(has_before)
    def _():
        greet({"seq": i - 1})
        greet({"seq": i - 1, "section": 1 - s})

    @pl.when(has_after)
    def _():
        greet({"seq": i + 1})
        greet({"seq": i + 1, "section": 1 - s})

    @pl.when(has_z_in)
    def _():
        greet({"seq": i - 2})

    @pl.when(has_z_out)
    def _():
        greet({"seq": i + 2})

    def remote(src, dst, send, recv, where):
        return pltpu.make_async_remote_copy(
            src_ref=src, dst_ref=dst, send_sem=send, recv_sem=recv,
            device_id=where, device_id_type=MESH,
        )

    def decay_copy(l):
        return remote(d_own.at[l], d_pair.at[l], d_sem.at[l, 0], d_sem.at[l, 1], {"seq": pair})

    def sum_copy(l):
        return remote(
            squares.at[l], sum_in.at[l], sum_sem.at[l, 0], sum_sem.at[l, 1], {"section": 1 - s}
        )

    def rows_copy(l):
        return remote(
            rows_out.at[l], rows_in.at[l], rows_sem.at[l, 0], rows_sem.at[l, 1], {"seq": i + 1}
        )

    def part_copy(l):
        return remote(
            part_out.at[l], part_in.at[l], part_sem.at[l, 0], part_sem.at[l, 1],
            {"seq": i + 1, "section": 1 - s},
        )

    def z_copy(l, c):
        return remote(
            z_out.at[l, c], z_in.at[l, c], z_send.at[l, c], z_recv.at[l, c], {"seq": i + 2}
        )

    def x_copy(l, c):
        return remote(
            x_out.at[l, c], x_in.at[l, c], x_send.at[l, c], x_recv.at[l, c], {"seq": pair}
        )

    def send_sums(l):
        part_out[l] = squares[l, length - 8 :, :]
        sum_copy(l).start()

        @pl.when(has_after)
        def _():
            rows_copy(l).start()
            part_copy(l).start()

    def fold(value):
        total = value[:, :128]
        for k in range(1, value.shape[1] // 128):
            total = total + value[:, k * 128 : (k + 1) * 128]
        return total

    squares[0] = jnp.zeros(squares.shape[1:], F32)
    arrivals[0].wait()

    @pl.loop(0, chunks)
    def _(c):
        h = prompt[:, cols(c)].astype(F32)
        squares[0] += fold(h * h)
        rows_out[0, :, cols(c)] = prompt[length - 16 :, cols(c)]

    @pl.when(i == 0)
    def _():
        rows_in[...] = jnp.zeros(rows_in.shape, BF16)
        part_in[...] = jnp.zeros(part_in.shape, F32)

    @pl.when(i < 2)
    def _():
        z_in[...] = jnp.zeros(z_in.shape, BF16)

    one = jnp.int32(1)
    zero = jnp.int32(0)
    expected = (
        1
        + 2 * jnp.where(has_before, one, zero)
        + 2 * jnp.where(has_after, one, zero)
        + jnp.where(has_z_in, one, zero)
        + jnp.where(has_z_out, one, zero)
    )
    pl.semaphore_wait(barrier, expected)
    send_sums(0)

    for k in range(1, len(arrivals)):
        arrivals[k].wait()

    def wide(pieces):
        lanes = sum(p.shape[1] for p in pieces)
        rest = jnp.zeros((pieces[0].shape[0], 128 - lanes), pieces[0].dtype)
        return jnp.concatenate(pieces + [rest], axis=1)

    idle = jnp.zeros((128 - layers * heads, length), F32)
    raw = jnp.concatenate([dt[l] for l in range(layers)] + [idle], axis=0).T
    rate = jnp.exp(wide([a_log[l : l + 1, :] for l in range(layers)])) * LOG2E
    delta = jnp.maximum(raw, 0.0) + jnp.log(1.0 + jnp.exp(-jnp.abs(raw)))
    step = -delta * rate
    t_of = lax.broadcasted_iota(jnp.int32, (length, length), 0)
    s_of = lax.broadcasted_iota(jnp.int32, (length, length), 1)
    lower = t_of >= s_of
    running = jnp.dot(
        lower.astype(F32), step, preferred_element_type=F32, precision=lax.Precision.HIGHEST
    )
    behind = running - jnp.log(delta) * LOG2E
    ahead = running[length - 1 :, :] - behind
    turned = behind.T
    for lc in range(layers * chunks):
        q_rows[lc, :per_chunk, :] = turned[lc * per_chunk : (lc + 1) * per_chunk, :]
    for l in range(layers):
        mine = slice(l * heads, (l + 1) * heads)
        r_split[l] = wide([p.astype(F32) for p in split3(running[:, mine])]).astype(BF16)
        f_split[l] = wide([p.astype(F32) for p in split3(ahead[:, mine])]).astype(BF16)

    def spread_steps(l, c):
        lc = l * chunks + c
        row = lax.broadcasted_iota(jnp.int32, (128, WIDE), 0)
        lane = lax.broadcasted_iota(jnp.int32, (128, WIDE), 1)
        hit = (lax.rem(row, heads) == c * per_chunk + lane // head_dim) & (row < 3 * heads)
        pick = hit.astype(F32).astype(BF16)
        spread = jnp.dot(r_split[l], pick, preferred_element_type=F32)
        r_exp[lc] = spread
        d_own[l, pl.ds(c, 1), :] = jnp.exp2(spread[length - 1 :, :])
        f_exp[lc] = jnp.exp2(jnp.dot(f_split[l], pick, preferred_element_type=F32))

    @pl.loop(0, chunks)
    def _(c):
        spread_steps(0, c)

    decay_copy(0).start()

    for l in range(layers):
        proj_wide[...] = proj[l].astype(F32)
        b_all = proj_wide[pl.ds(0, length, stride=2), :]
        c_all = proj_wide[pl.ds(1, length, stride=2), :]
        turned_b = b_all.T.astype(BF16)
        b_t[l] = turned_b
        for g in range(groups):
            c_g = c_all[:, g * STATE : (g + 1) * STATE]
            c_two[l * groups + g] = jnp.concatenate([c_g, c_g], axis=1).astype(BF16)
            both = jnp.dot(
                c_g.astype(BF16), turned_b[g * STATE : (g + 1) * STATE], preferred_element_type=F32
            )
            scores[l * groups + g] = jnp.where(lower, both, 0.0)

    head_of = lax.broadcasted_iota(jnp.int32, (length, WIDE), 1) // head_dim

    for l in range(layers):
        sum_copy(l).wait_recv()
        total = jnp.sum(squares[l] + sum_in[l], axis=1, keepdims=True)
        scale[...] = jnp.broadcast_to(
            lax.rsqrt(total / (width * sections) + EPSILON), scale.shape
        )

        @pl.when(has_before)
        def _():
            rows_copy(l).wait_recv()
            part_copy(l).wait_recv()

        halo_sum = part_in[l]
        for c in range(chunks):
            h = rows_in[l, :, c * WIDE : (c + 1) * WIDE].astype(F32)[8:]
            halo_sum = halo_sum + fold(h * h)
        halo_total = jnp.sum(halo_sum, axis=1, keepdims=True)
        scale_halo[...] = jnp.broadcast_to(
            lax.rsqrt(halo_total / (width * sections) + EPSILON), scale_halo.shape
        )
        decay_copy(l).wait_recv()

        def source(c):
            return prompt[:, cols(c)] if l == 0 else out[l - 1, :, cols(c)]

        def double(value):
            return jnp.concatenate([value] * (WIDE // 128), axis=1)

        def coefficients(c):
            own = d_own[l, pl.ds(c, 1), :]
            other = d_pair[l, pl.ds(c, 1), :]
            return own, other

        @pl.loop(0, chunks)
        def _(c):
            gain = gain_in[l : l + 1, cols(c)]
            h = source(c).astype(F32)
            normed = (h * double(scale[...]) * gain).astype(BF16).astype(F32)
            before = rows_in[l, :, cols(c)].astype(F32)[8:]
            pad[:8, :] = (before * double(scale_halo[...]) * gain).astype(BF16).astype(F32)
            pad[8:, :] = normed
            weight = conv_w[l, :, cols(c)].astype(F32)
            total = weight[taps - 1 : taps, :] * normed
            for k in range(taps - 1):
                start = 8 - (taps - 1) + k
                total = total + weight[k : k + 1, :] * pad[start : start + length, :]
            half = 0.5 * total
            here = (half + half * jnp.tanh(half)).astype(BF16)
            mixed[c] = here
            scaled = (f_exp[l * chunks + c] * here.astype(F32)).astype(BF16)
            g = c // per_group
            rows = pl.ds(pl.multiple_of(g * STATE, STATE), STATE)
            state = jnp.dot(b_t[l, rows, :], scaled, preferred_element_type=F32)
            local[c] = state
            own, other = coefficients(c)

            @pl.when(i < 2)
            def _():
                z_out[l, c] = (jnp.where(first, other, 1.0) * state).astype(BF16)

                @pl.when(has_z_out)
                def _():
                    z_copy(l, c).start()

        if l + 1 < layers:
            squares[l + 1] = jnp.zeros(squares.shape[1:], F32)

        def finish(c):
            x_copy(l, c).wait_recv()
            own, other = coefficients(c)
            g = l * groups + c // per_group
            entering = jnp.where(first, 1.0, other) * z_in[l, c].astype(F32) + x_in[l, c].astype(F32)
            high = entering.astype(BF16)
            low = (entering - high.astype(F32)).astype(BF16)
            inter = jnp.dot(
                c_two[g], jnp.concatenate([high, low], axis=0), preferred_element_type=F32
            )
            y = intra[c] + jnp.exp2(r_exp[l * chunks + c]) * inter
            row = lax.broadcasted_iota(jnp.int32, (WIDE, WIDE), 0) // head_dim
            same = (row == lax.broadcasted_iota(jnp.int32, (WIDE, WIDE), 1) // head_dim)
            power = jnp.dot(
                (y * y).astype(BF16), same.astype(F32).astype(BF16), preferred_element_type=F32
            )
            scaled = y * lax.rsqrt(power * (1.0 / head_dim) + EPSILON)
            after = (source(c).astype(F32) + scaled * gain_out[l : l + 1, cols(c)]).astype(BF16)
            out[l, :, cols(c)] = after
            if l + 1 < layers:
                rows_out[l + 1, :, cols(c)] = after[length - 16 :, :]
                wide_after = after.astype(F32)
                squares[l + 1] += fold(wide_after * wide_after)

        @pl.loop(0, chunks)
        def _(c):
            lc = l * chunks + c
            g = l * groups + c // per_group
            here = mixed[c]
            left, right = [], []
            for h in range(per_chunk):
                column = r_exp[lc, :, h * head_dim : h * head_dim + 1]
                decay = jnp.exp2(column - q_rows[lc, h : h + 1, :])
                left.append((decay * scores[g]).astype(BF16))
                right.append(jnp.where(head_of == h, here, jnp.zeros_like(here)))
            intra[c] = jnp.dot(
                jnp.concatenate(left, axis=1),
                jnp.concatenate(right, axis=0),
                preferred_element_type=F32,
            )
            own, other = coefficients(c)
            state = local[c]

            @pl.when(has_z_in)
            def _():
                z_copy(l, c).wait_recv()

                @pl.when(has_z_out)
                def _():
                    z_out[l, c] = (
                        own * other * z_in[l, c].astype(F32) + jnp.where(first, other, 1.0) * state
                    ).astype(BF16)
                    z_copy(l, c).start()

            arrived = z_in[l, c].astype(F32)
            x_out[l, c] = jnp.where(first, own * arrived + state, arrived).astype(BF16)
            x_copy(l, c).start()

            if l + 1 < layers:
                spread_steps(l + 1, c)

        if l + 1 < layers:
            decay_copy(l + 1).start()

        @pl.loop(0, chunks)
        def _(c):
            finish(c)

        if l + 1 < layers:
            send_sums(l + 1)

    for l in range(layers):
        decay_copy(l).wait_send()
        sum_copy(l).wait_send()

        @pl.when(has_after)
        def _():
            rows_copy(l).wait_send()
            part_copy(l).wait_send()

        @pl.loop(0, chunks)
        def _(c):
            x_copy(l, c).wait_send()

            @pl.when(has_z_out)
            def _():
                z_copy(l, c).wait_send()


def local_part(n, sections, prompt, in_gain, conv_w, a_log, out_gain, dt_raw, proj):
    length, width = prompt.shape
    layers, _, heads = dt_raw.shape
    operands = (
        prompt, in_gain, conv_w, a_log, out_gain,
        dt_raw.transpose(0, 2, 1), proj.reshape(layers, 2 * length, proj.shape[3]),
    )
    chunks = width // WIDE
    groups = proj.shape[3] // STATE
    vmem = pltpu.VMEM
    dma = pltpu.SemaphoreType.DMA
    lc = layers * chunks
    scratch = [vmem(value.shape, value.dtype) for value in operands] + [
        vmem((2 * length, proj.shape[3]), F32),
        dma((len(operands),)),
        vmem((layers, length, 128), BF16),
        vmem((layers, length, 128), BF16),
        vmem((lc, length, WIDE), F32),
        vmem((lc, length, WIDE), F32),
        vmem((lc, 8, length), F32),
        vmem((layers * groups, length, length), F32),
        vmem((layers, groups * STATE, length), BF16),
        vmem((layers * groups, length, 2 * STATE), BF16),
        vmem((length + 8, WIDE), F32),
        vmem((chunks, length, WIDE), BF16),
        vmem((chunks, length, WIDE), F32),
        vmem((chunks, STATE, WIDE), F32),
        vmem((layers, length, 128), F32),
        vmem((length, 128), F32),
        vmem((8, 128), F32),
        vmem((layers, chunks, WIDE), F32),
        vmem((layers, chunks, WIDE), F32),
        vmem((layers, length, 128), F32),
        vmem((layers, 16, width), BF16),
        vmem((layers, 16, width), BF16),
        vmem((layers, 8, 128), F32),
        vmem((layers, 8, 128), F32),
        vmem((layers, chunks, STATE, WIDE), BF16),
        vmem((layers, chunks, STATE, WIDE), BF16),
        vmem((layers, chunks, STATE, WIDE), BF16),
        vmem((layers, chunks, STATE, WIDE), BF16),
        dma((layers, 2)),
        dma((layers, 2)),
        dma((layers, 2)),
        dma((layers, 2)),
        dma((layers, chunks)),
        dma((layers, chunks)),
        dma((layers, chunks)),
        dma((layers, chunks)),
    ]
    return pl.pallas_call(
        functools.partial(kernel, n, sections),
        out_shape=pltpu.VMEM((layers, length, width), BF16),
        in_specs=[pl.BlockSpec(memory_space=pltpu.HBM)] * len(operands),
        out_specs=pl.BlockSpec(memory_space=pltpu.VMEM),
        scratch_shapes=scratch,
        compiler_params=pltpu.CompilerParams(
            collective_id=0, has_side_effects=True, vmem_limit_bytes=60 * 1024 * 1024
        ),
    )(*operands)


def solution(mesh):
    in_specs = (
        P(("groups", "seq"), "section"),
        P(None, "section"),
        P(None, None, "section"),
        P(None, "section"),
        P(None, "section"),
        P(None, ("groups", "seq"), "section"),
        P(None, ("groups", "seq"), None, "section"),
    )
    out_specs = P(None, ("groups", "seq"), "section")
    part = functools.partial(local_part, mesh.shape["seq"], mesh.shape["section"])
    return jax.shard_map(part, mesh=mesh, in_specs=in_specs, out_specs=out_specs, check_vma=False)
```

```python
import functools

import jax
import jax.numpy as jnp
from jax import lax
from jax.experimental import pallas as pl
from jax.experimental.pallas import tpu as pltpu
from jax.sharding import PartitionSpec as P

STATE = 64
WIDE = 256
EPSILON = 1e-05
LOG2E = 1.4426950408889634
MESH = pl.DeviceIdType.MESH
F32 = jnp.float32
BF16 = jnp.bfloat16


def split3(value):
    high = value.astype(BF16)
    rest = value - high.astype(F32)
    middle = rest.astype(BF16)
    low = (rest - middle.astype(F32)).astype(BF16)
    return high, middle, low


def kernel(
    n, sections, prompt_h, gain_in_h, conv_w_h, a_log_h, gain_out_h, dt_h, proj_h, out,
    prompt, gain_in, conv_w, a_log, gain_out, dt, proj, proj_wide, in_sem,
    r_split, f_split, r_exp, f_exp, q_rows, scores, b_t, c_two,
    pad, mixed, intra, local, squares, scale, scale_halo,
    d_own, d_pair, sum_in, rows_out, rows_in, part_out, part_in,
    z_out, z_in, x_out, x_in,
    d_sem, sum_sem, rows_sem, part_sem, z_send, z_recv, x_send, x_recv,
):
    layers, heads, length = dt.shape
    width = prompt.shape[1]
    head_dim = width // heads
    chunks = width // WIDE
    per_chunk = WIDE // head_dim
    groups = proj.shape[2] // STATE
    per_group = chunks // groups
    taps = conv_w.shape[1]

    i = lax.axis_index("seq")
    s = lax.axis_index("section")
    pair = i + 1 - 2 * lax.rem(i, 2)
    first = lax.rem(i, 2) == 0
    has_before = i >= 1
    has_after = i < n - 1
    has_z_in = i >= 2
    has_z_out = i < n - 2

    def cols(c):
        return pl.ds(pl.multiple_of(c * WIDE, WIDE), WIDE)

    arrivals = {}
    for k, (there, here) in enumerate(
        (
            (prompt_h, prompt), (dt_h, dt), (a_log_h, a_log), (proj_h, proj),
            (gain_in_h, gain_in), (conv_w_h, conv_w), (gain_out_h, gain_out),
        )
    ):
        arrivals[k] = pltpu.make_async_copy(there, here, in_sem.at[k])
        arrivals[k].start()

    barrier = pltpu.get_barrier_semaphore()

    def greet(where):
        pl.semaphore_signal(barrier, inc=1, device_id=where, device_id_type=MESH)

    greet({"section": 1 - s})

    @pl.when(has_before)
    def _():
        greet({"seq": i - 1})
        greet({"seq": i - 1, "section": 1 - s})

    @pl.when(has_after)
    def _():
        greet({"seq": i + 1})
        greet({"seq": i + 1, "section": 1 - s})

    @pl.when(has_z_in)
    def _():
        greet({"seq": i - 2})

    @pl.when(has_z_out)
    def _():
        greet({"seq": i + 2})

    def remote(src, dst, send, recv, where):
        return pltpu.make_async_remote_copy(
            src_ref=src, dst_ref=dst, send_sem=send, recv_sem=recv,
            device_id=where, device_id_type=MESH,
        )

    def decay_copy(l):
        return remote(d_own.at[l], d_pair.at[l], d_sem.at[l, 0], d_sem.at[l, 1], {"seq": pair})

    def sum_copy(l):
        return remote(
            squares.at[l], sum_in.at[l], sum_sem.at[l, 0], sum_sem.at[l, 1], {"section": 1 - s}
        )

    def rows_copy(l):
        return remote(
            rows_out.at[l], rows_in.at[l], rows_sem.at[l, 0], rows_sem.at[l, 1], {"seq": i + 1}
        )

    def part_copy(l):
        return remote(
            part_out.at[l], part_in.at[l], part_sem.at[l, 0], part_sem.at[l, 1],
            {"seq": i + 1, "section": 1 - s},
        )

    def z_copy(l, c):
        return remote(
            z_out.at[l, c], z_in.at[l, c], z_send.at[l, c], z_recv.at[l, c], {"seq": i + 2}
        )

    def x_copy(l, c):
        return remote(
            x_out.at[l, c], x_in.at[l, c], x_send.at[l, c], x_recv.at[l, c], {"seq": pair}
        )

    def send_sums(l):
        part_out[l] = squares[l, length - 8 :, :]
        sum_copy(l).start()

        @pl.when(has_after)
        def _():
            rows_copy(l).start()
            part_copy(l).start()

    def fold(value):
        total = value[:, :128]
        for k in range(1, value.shape[1] // 128):
            total = total + value[:, k * 128 : (k + 1) * 128]
        return total

    squares[0] = jnp.zeros(squares.shape[1:], F32)
    arrivals[0].wait()

    @pl.loop(0, chunks)
    def _(c):
        h = prompt[:, cols(c)].astype(F32)
        squares[0] += fold(h * h)
        rows_out[0, :, cols(c)] = prompt[length - 16 :, cols(c)]

    @pl.when(i == 0)
    def _():
        rows_in[...] = jnp.zeros(rows_in.shape, BF16)
        part_in[...] = jnp.zeros(part_in.shape, F32)

    @pl.when(i < 2)
    def _():
        z_in[...] = jnp.zeros(z_in.shape, BF16)

    one = jnp.int32(1)
    zero = jnp.int32(0)
    expected = (
        1
        + 2 * jnp.where(has_before, one, zero)
        + 2 * jnp.where(has_after, one, zero)
        + jnp.where(has_z_in, one, zero)
        + jnp.where(has_z_out, one, zero)
    )

    for k in range(1, len(arrivals)):
        arrivals[k].wait()

    def wide(pieces):
        lanes = sum(p.shape[1] for p in pieces)
        rest = jnp.zeros((pieces[0].shape[0], 128 - lanes), pieces[0].dtype)
        return jnp.concatenate(pieces + [rest], axis=1)

    idle = jnp.zeros((128 - layers * heads, length), F32)
    raw = jnp.concatenate([dt[l] for l in range(layers)] + [idle], axis=0).T
    rate = jnp.exp(wide([a_log[l : l + 1, :] for l in range(layers)])) * LOG2E
    delta = jnp.maximum(raw, 0.0) + jnp.log(1.0 + jnp.exp(-jnp.abs(raw)))
    step = -delta * rate
    t_of = lax.broadcasted_iota(jnp.int32, (length, length), 0)
    s_of = lax.broadcasted_iota(jnp.int32, (length, length), 1)
    lower = t_of >= s_of
    running = jnp.dot(
        lower.astype(F32), step, preferred_element_type=F32, precision=lax.Precision.HIGHEST
    )
    behind = running - jnp.log(delta) * LOG2E
    ahead = running[length - 1 :, :] - behind
    turned = behind.T
    for lc in range(layers * chunks):
        q_rows[lc, :per_chunk, :] = turned[lc * per_chunk : (lc + 1) * per_chunk, :]
    for l in range(layers):
        mine = slice(l * heads, (l + 1) * heads)
        r_split[l] = wide([p.astype(F32) for p in split3(running[:, mine])]).astype(BF16)
        f_split[l] = wide([p.astype(F32) for p in split3(ahead[:, mine])]).astype(BF16)

    def spread_steps(l, c):
        lc = l * chunks + c
        row = lax.broadcasted_iota(jnp.int32, (128, WIDE), 0)
        lane = lax.broadcasted_iota(jnp.int32, (128, WIDE), 1)
        hit = (lax.rem(row, heads) == c * per_chunk + lane // head_dim) & (row < 3 * heads)
        pick = hit.astype(F32).astype(BF16)
        spread = jnp.dot(r_split[l], pick, preferred_element_type=F32)
        r_exp[lc] = spread
        d_own[l, pl.ds(c, 1), :] = jnp.exp2(spread[length - 1 :, :])
        f_exp[lc] = jnp.exp2(jnp.dot(f_split[l], pick, preferred_element_type=F32))

    pl.semaphore_wait(barrier, expected)
    send_sums(0)

    @pl.loop(0, chunks)
    def _(c):
        spread_steps(0, c)

    decay_copy(0).start()

    for l in range(layers):
        proj_wide[...] = proj[l].astype(F32)
        b_all = proj_wide[pl.ds(0, length, stride=2), :]
        c_all = proj_wide[pl.ds(1, length, stride=2), :]
        turned_b = b_all.T.astype(BF16)
        b_t[l] = turned_b
        for g in range(groups):
            c_g = c_all[:, g * STATE : (g + 1) * STATE]
            c_two[l * groups + g] = jnp.concatenate([c_g, c_g], axis=1).astype(BF16)
            both = jnp.dot(
                c_g.astype(BF16), turned_b[g * STATE : (g + 1) * STATE], preferred_element_type=F32
            )
            scores[l * groups + g] = jnp.where(lower, both, 0.0)

    head_of = lax.broadcasted_iota(jnp.int32, (length, WIDE), 1) // head_dim

    for l in range(layers):
        sum_copy(l).wait_recv()
        total = jnp.sum(squares[l] + sum_in[l], axis=1, keepdims=True)
        scale[...] = jnp.broadcast_to(
            lax.rsqrt(total / (width * sections) + EPSILON), scale.shape
        )

        @pl.when(has_before)
        def _():
            rows_copy(l).wait_recv()
            part_copy(l).wait_recv()

        halo_sum = part_in[l]
        for c in range(chunks):
            h = rows_in[l, :, c * WIDE : (c + 1) * WIDE].astype(F32)[8:]
            halo_sum = halo_sum + fold(h * h)
        halo_total = jnp.sum(halo_sum, axis=1, keepdims=True)
        scale_halo[...] = jnp.broadcast_to(
            lax.rsqrt(halo_total / (width * sections) + EPSILON), scale_halo.shape
        )
        decay_copy(l).wait_recv()

        def source(c):
            return prompt[:, cols(c)] if l == 0 else out[l - 1, :, cols(c)]

        def double(value):
            return jnp.concatenate([value] * (WIDE // 128), axis=1)

        def coefficients(c):
            own = d_own[l, pl.ds(c, 1), :]
            other = d_pair[l, pl.ds(c, 1), :]
            return own, other

        @pl.loop(0, chunks)
        def _(c):
            gain = gain_in[l : l + 1, cols(c)]
            h = source(c).astype(F32)
            normed = (h * double(scale[...]) * gain).astype(BF16).astype(F32)
            before = rows_in[l, :, cols(c)].astype(F32)[8:]
            pad[:8, :] = (before * double(scale_halo[...]) * gain).astype(BF16).astype(F32)
            pad[8:, :] = normed
            weight = conv_w[l, :, cols(c)].astype(F32)
            total = weight[taps - 1 : taps, :] * normed
            for k in range(taps - 1):
                start = 8 - (taps - 1) + k
                total = total + weight[k : k + 1, :] * pad[start : start + length, :]
            half = 0.5 * total
            here = (half + half * jnp.tanh(half)).astype(BF16)
            mixed[c] = here
            scaled = (f_exp[l * chunks + c] * here.astype(F32)).astype(BF16)
            g = c // per_group
            rows = pl.ds(pl.multiple_of(g * STATE, STATE), STATE)
            state = jnp.dot(b_t[l, rows, :], scaled, preferred_element_type=F32)
            local[c] = state
            own, other = coefficients(c)

            @pl.when(i < 2)
            def _():
                z_out[l, c] = (jnp.where(first, other, 1.0) * state).astype(BF16)

                @pl.when(has_z_out)
                def _():
                    z_copy(l, c).start()

        if l + 1 < layers:
            squares[l + 1] = jnp.zeros(squares.shape[1:], F32)

        def finish(c):
            x_copy(l, c).wait_recv()
            own, other = coefficients(c)
            g = l * groups + c // per_group
            entering = jnp.where(first, 1.0, other) * z_in[l, c].astype(F32) + x_in[l, c].astype(F32)
            high = entering.astype(BF16)
            low = (entering - high.astype(F32)).astype(BF16)
            inter = jnp.dot(
                c_two[g], jnp.concatenate([high, low], axis=0), preferred_element_type=F32
            )
            y = intra[c] + jnp.exp2(r_exp[l * chunks + c]) * inter
            row = lax.broadcasted_iota(jnp.int32, (WIDE, WIDE), 0) // head_dim
            same = (row == lax.broadcasted_iota(jnp.int32, (WIDE, WIDE), 1) // head_dim)
            power = jnp.dot(
                (y * y).astype(BF16), same.astype(F32).astype(BF16), preferred_element_type=F32
            )
            scaled = y * lax.rsqrt(power * (1.0 / head_dim) + EPSILON)
            after = (source(c).astype(F32) + scaled * gain_out[l : l + 1, cols(c)]).astype(BF16)
            out[l, :, cols(c)] = after
            if l + 1 < layers:
                rows_out[l + 1, :, cols(c)] = after[length - 16 :, :]
                wide_after = after.astype(F32)
                squares[l + 1] += fold(wide_after * wide_after)

        @pl.loop(0, chunks)
        def _(c):
            own, other = coefficients(c)
            state = local[c]

            @pl.when(has_z_in)
            def _():
                z_copy(l, c).wait_recv()

                @pl.when(has_z_out)
                def _():
                    z_out[l, c] = (
                        own * other * z_in[l, c].astype(F32) + jnp.where(first, other, 1.0) * state
                    ).astype(BF16)
                    z_copy(l, c).start()

            arrived = z_in[l, c].astype(F32)
            x_out[l, c] = jnp.where(first, own * arrived + state, arrived).astype(BF16)
            x_copy(l, c).start()

            lc = l * chunks + c
            g = l * groups + c // per_group
            here = mixed[c]
            left, right = [], []
            for h in range(per_chunk):
                column = r_exp[lc, :, h * head_dim : h * head_dim + 1]
                decay = jnp.exp2(column - q_rows[lc, h : h + 1, :])
                left.append((decay * scores[g]).astype(BF16))
                right.append(jnp.where(head_of == h, here, jnp.zeros_like(here)))
            intra[c] = jnp.dot(
                jnp.concatenate(left, axis=1),
                jnp.concatenate(right, axis=0),
                preferred_element_type=F32,
            )

        if l + 1 < layers:
            @pl.loop(0, chunks)
            def _(c):
                spread_steps(l + 1, c)

            decay_copy(l + 1).start()

        @pl.loop(0, chunks)
        def _(c):
            finish(c)

        if l + 1 < layers:
            send_sums(l + 1)

    for l in range(layers):
        decay_copy(l).wait_send()
        sum_copy(l).wait_send()

        @pl.when(has_after)
        def _():
            rows_copy(l).wait_send()
            part_copy(l).wait_send()

        @pl.loop(0, chunks)
        def _(c):
            x_copy(l, c).wait_send()

            @pl.when(has_z_out)
            def _():
                z_copy(l, c).wait_send()


def local_part(n, sections, prompt, in_gain, conv_w, a_log, out_gain, dt_raw, proj):
    length, width = prompt.shape
    layers, _, heads = dt_raw.shape
    operands = (
        prompt, in_gain, conv_w, a_log, out_gain,
        dt_raw.transpose(0, 2, 1), proj.reshape(layers, 2 * length, proj.shape[3]),
    )
    chunks = width // WIDE
    groups = proj.shape[3] // STATE
    vmem = pltpu.VMEM
    dma = pltpu.SemaphoreType.DMA
    lc = layers * chunks
    scratch = [vmem(value.shape, value.dtype) for value in operands] + [
        vmem((2 * length, proj.shape[3]), F32),
        dma((len(operands),)),
        vmem((layers, length, 128), BF16),
        vmem((layers, length, 128), BF16),
        vmem((lc, length, WIDE), F32),
        vmem((lc, length, WIDE), F32),
        vmem((lc, 8, length), F32),
        vmem((layers * groups, length, length), F32),
        vmem((layers, groups * STATE, length), BF16),
        vmem((layers * groups, length, 2 * STATE), BF16),
        vmem((length + 8, WIDE), F32),
        vmem((chunks, length, WIDE), BF16),
        vmem((chunks, length, WIDE), F32),
        vmem((chunks, STATE, WIDE), F32),
        vmem((layers, length, 128), F32),
        vmem((length, 128), F32),
        vmem((8, 128), F32),
        vmem((layers, chunks, WIDE), F32),
        vmem((layers, chunks, WIDE), F32),
        vmem((layers, length, 128), F32),
        vmem((layers, 16, width), BF16),
        vmem((layers, 16, width), BF16),
        vmem((layers, 8, 128), F32),
        vmem((layers, 8, 128), F32),
        vmem((layers, chunks, STATE, WIDE), BF16),
        vmem((layers, chunks, STATE, WIDE), BF16),
        vmem((layers, chunks, STATE, WIDE), BF16),
        vmem((layers, chunks, STATE, WIDE), BF16),
        dma((layers, 2)),
        dma((layers, 2)),
        dma((layers, 2)),
        dma((layers, 2)),
        dma((layers, chunks)),
        dma((layers, chunks)),
        dma((layers, chunks)),
        dma((layers, chunks)),
    ]
    return pl.pallas_call(
        functools.partial(kernel, n, sections),
        out_shape=pltpu.VMEM((layers, length, width), BF16),
        in_specs=[pl.BlockSpec(memory_space=pltpu.HBM)] * len(operands),
        out_specs=pl.BlockSpec(memory_space=pltpu.VMEM),
        scratch_shapes=scratch,
        compiler_params=pltpu.CompilerParams(
            collective_id=0, has_side_effects=True, vmem_limit_bytes=60 * 1024 * 1024
        ),
    )(*operands)


def solution(mesh):
    in_specs = (
        P(("groups", "seq"), "section"),
        P(None, "section"),
        P(None, None, "section"),
        P(None, "section"),
        P(None, "section"),
        P(None, ("groups", "seq"), "section"),
        P(None, ("groups", "seq"), None, "section"),
    )
    out_specs = P(None, ("groups", "seq"), "section")
    part = functools.partial(local_part, mesh.shape["seq"], mesh.shape["section"])
    return jax.shard_map(part, mesh=mesh, in_specs=in_specs, out_specs=out_specs, check_vma=False)
```
